32 devices in a mesh: bag: 4 (over y, core), head: 8 (over z, x).
Axes of the slice: x: 2, y: 2, z: 4, core: 2. Of those that a mesh axis runs over, the one named last changes fastest.
Arguments:
- dout: bfloat16 [4096, 6144], P(('bag', 'head')), may hold values from -6 to 6
- destination: int32 [4096], P(('bag', 'head')), may hold values from 0 to 4095, as said below
- q_bag: bfloat16 [4096, 6144], P(('bag', 'head')), may hold values from -32 to 32
- k_bag: bfloat16 [4096, 6144], P(('bag', 'head')), may hold values from -32 to 32
- v_bag: bfloat16 [4096, 6144], P(('bag', 'head')), may hold values from -6 to 6
- seq_ids: int32 [4, 1024], P('bag'), may hold values from 0 to 2, never falling along the last dimension, each value on 1 to 768 neighbouring positions
Outputs:
- dq_bag: bfloat16 [4096, 6144], P(('bag', 'head'))
- dk_bag: bfloat16 [4096, 6144], P(('bag', 'head'))
- dv_bag: bfloat16 [4096, 6144], P(('bag', 'head'))
The draws below stay inside these ranges and needn't reach their ends.
Inputs may be any that keep to these rules, and one draw needn't show every extreme that they name: destination is a permutation. A row at home index i goes to a bag row held at the same index along head: destination // 128 % 8 equals i // 128 % 8. The rows of one device go to at most four bags, at most 64 of them to one bag, and in every draw some device sends exactly 64 rows to some bag.
All inputs are finite; a program needn't handle non-finite values.
Results may differ from the reference program's by a relative error of at most 0.011.
Values may be sent and summed in bfloat16 or wider, within the bound.
A program may use at most 128 MiB of HBM per device.

```python
import math
import jax
import jax.numpy as jnp
import numpy as np
from jax import lax

HEADS = 48
HEAD_DIM = 128
ROWS_DEV = 128
SEQS = 3
W = 6144
BAG_ROWS = 1024
TOKENS = 4096
CAP = 64
SEQ_MOST = 768
N_BAG = 4
N_HEAD = 8


def draw_destination(key, part):
    key = jax.random.fold_in(key, 7)
    remain = ROWS_DEV - CAP

    def column(column_key):
        keys = jax.random.split(column_key, 5)
        shifts = jax.random.permutation(keys[0], N_BAG)[:4]
        first = jax.random.randint(keys[1], (), 1, remain - 1)
        second = jax.random.randint(keys[2], (), 1, remain - first)
        bounds = jnp.stack([CAP, CAP + first, CAP + first + second])
        places = jnp.arange(ROWS_DEV)
        group = jnp.sum((places[:, None] >= bounds[None, :]).astype(jnp.int32), axis=1)
        source_perm = jax.vmap(lambda k: jax.random.permutation(k, ROWS_DEV))(jax.random.split(keys[3], N_BAG))
        target_perm = jax.vmap(lambda k: jax.random.permutation(k, ROWS_DEV))(jax.random.split(keys[4], N_BAG))
        bag_list = jnp.arange(N_BAG)
        target = (bag_list[:, None] + shifts[group][None, :]) % N_BAG
        slot_at = target_perm[target, places[None, :]]
        target_row = jnp.zeros((N_BAG, ROWS_DEV), jnp.int32).at[bag_list[:, None], source_perm].set(target)
        slot_row = jnp.zeros((N_BAG, ROWS_DEV), jnp.int32).at[bag_list[:, None], source_perm].set(slot_at)
        return (target_row, slot_row)
    targets, slots = jax.vmap(column)(jax.random.split(key, N_HEAD))
    head_list = jnp.arange(N_HEAD)[:, None, None]
    dest = (targets * N_HEAD + head_list) * ROWS_DEV + slots
    return dest.transpose(1, 0, 2).reshape(-1).astype(jnp.int32)


def draw_q_bag(key, part):
    jitter = jnp.clip(jax.random.normal(jax.random.fold_in(key, 31), (TOKENS, HEADS * HEAD_DIM)), -6.0, 6.0)
    return jitter.astype(jnp.bfloat16)


def draw_k_bag(key, part):
    jitter = jnp.clip(jax.random.normal(jax.random.fold_in(key, 33), (TOKENS, HEADS * HEAD_DIM)), -6.0, 6.0)
    return jitter.astype(jnp.bfloat16)


def block_levels(own_key, shape, pieces, low, high):
    loudness = 1.0
    for axis_at, shards_of in pieces:
        draws = jax.random.uniform(jax.random.fold_in(jax.random.fold_in(own_key, 6), axis_at), (shards_of,), jnp.float32, low / len(pieces), high / len(pieces))
        loudness = loudness * jnp.repeat(jnp.exp(draws), shape[axis_at] // shards_of).reshape((-1,) + (1,) * (len(shape) - 1 - axis_at))
    return loudness


def split_up(count, total, reach, lean):
    loads = [(1 << 20) // math.isqrt(standing ** lean) + 1 for standing in range(2, count + 1)]
    spare, given = total - reach - (count - 1), [1] * (count - 1)
    while spare > 0:
        movable = [i for i in range(count - 1) if given[i] < reach]
        pool, budget = sum([loads[i] for i in movable]), spare
        for i in movable:
            addition = min(reach - given[i], max(1, budget * loads[i] // pool), spare)
            given[i] = given[i] + addition
            spare = spare - addition
    return np.array([reach] + given)


def ragged(rng, number_of, total, most, slope):
    if number_of == 2:
        one = jax.random.randint(rng, (), max(1, total - most), min(most, total - 1) + 1)
        return jnp.stack([one, total - one])
    tallies = jnp.asarray(split_up(number_of, total, most, slope), jnp.int32)
    couples = (number_of - 1) // 2
    giver, sink = tallies[1:1 + 2 * couples:2], tallies[2:2 + 2 * couples:2]
    slack = jnp.minimum(giver - 1, most - sink)
    moved = jax.random.randint(jax.random.fold_in(rng, 1), (couples,), 0, 1 << 20) % (slack + 1)
    tallies = tallies.at[1:1 + 2 * couples:2].set(giver - moved).at[2:2 + 2 * couples:2].set(sink + moved)
    return tallies[jax.random.permutation(jax.random.fold_in(rng, 2), number_of)]


def noise(stream_key, extent, deviation, bound, pieces=(), kind=jnp.bfloat16):
    factor_of = block_levels(stream_key, extent, pieces, -0.22, 0.18) if pieces else 1.0
    values = jax.random.normal(stream_key, extent, jnp.float32) * deviation * factor_of
    return jnp.minimum(jnp.maximum(values, -bound), bound).astype(kind)


def setup_inputs(seed: int = 0) -> dict:
    splits = jax.random.split(jax.random.key(seed), 7)
    return {
        "dout": noise(splits[0], (TOKENS, W), 1.0, 6.0, ((0, 32),)),
        "destination": draw_destination(jax.random.fold_in(splits[6], 71), 0),
        "q_bag": draw_q_bag(jax.random.fold_in(splits[6], 71), 0),
        "k_bag": draw_k_bag(jax.random.fold_in(splits[6], 71), 0),
        "v_bag": noise(splits[4], (TOKENS, W), 1.0, 6.0, ((0, 32),)),
        "seq_ids": jax.vmap(lambda own: jnp.searchsorted(jnp.cumsum(ragged(own, SEQS, BAG_ROWS, SEQ_MOST, 1)), jnp.arange(BAG_ROWS), side="right"))(jax.random.split(splits[5], N_BAG)).reshape((N_BAG, BAG_ROWS)).astype(jnp.int32),
    }


def head_backward(operands, seq_labels):
    query, keys, values, grad_out = operands
    score_scale = HEAD_DIM ** -0.5
    scores = jnp.dot(query, keys.T, preferred_element_type=jnp.float32) * score_scale
    same_seq = seq_labels[:, None] == seq_labels[None, :]
    scores = jnp.where(same_seq, scores, -jnp.inf)
    row_top = jnp.max(scores, axis=-1, keepdims=True)
    exponent = jnp.exp(scores - row_top)
    softmax_rows = exponent / jnp.sum(exponent, axis=-1, keepdims=True)
    probs_low = softmax_rows.astype(jnp.bfloat16)
    grad_values = jnp.dot(probs_low.T, grad_out, preferred_element_type=jnp.float32).astype(jnp.bfloat16)
    grad_probs = jnp.dot(grad_out, values.T, preferred_element_type=jnp.float32)
    delta = jnp.sum(softmax_rows * grad_probs, axis=-1, keepdims=True)
    grad_scores = (softmax_rows * (grad_probs - delta) * score_scale).astype(jnp.bfloat16)
    grad_query = jnp.dot(grad_scores, keys, preferred_element_type=jnp.float32).astype(jnp.bfloat16)
    grad_keys = jnp.dot(grad_scores.T, query, preferred_element_type=jnp.float32).astype(jnp.bfloat16)
    return grad_query, grad_keys, grad_values


def reference(dout, destination, q_bag, k_bag, v_bag, seq_ids):
    dout_bag = jnp.zeros_like(dout).at[destination].set(dout)
    bag_rows = TOKENS // N_BAG

    def split_heads(array, bag_number):
        piece = lax.dynamic_slice_in_dim(array, bag_number * bag_rows, bag_rows, 0)
        return piece.reshape(bag_rows, HEADS, HEAD_DIM).transpose(1, 0, 2)

    def one_bag(bag_number):
        seq_labels = seq_ids[bag_number]
        operands = (split_heads(q_bag, bag_number), split_heads(k_bag, bag_number),
                    split_heads(v_bag, bag_number), split_heads(dout_bag, bag_number))
        grads = lax.map(lambda item: head_backward(item, seq_labels), operands)
        return tuple(g.transpose(1, 0, 2).reshape(bag_rows, HEADS * HEAD_DIM) for g in grads)

    grad_q, grad_k, grad_v = lax.map(one_bag, jnp.arange(N_BAG, dtype=jnp.int32))
    full_width = HEADS * HEAD_DIM
    return (grad_q.reshape(TOKENS, full_width), grad_k.reshape(TOKENS, full_width),
            grad_v.reshape(TOKENS, full_width))
```

```python
import functools

import jax
import jax.numpy as jnp
from jax import lax
from jax.experimental import pallas as pl
from jax.experimental.pallas import tpu as pltpu
from jax.sharding import PartitionSpec as P

HEAD_DIM = 128
CAP = 64
MESH = pl.DeviceIdType.MESH
F32 = jnp.float32
BF16 = jnp.bfloat16
CONTRACT_LAST = (((1,), (1,)), ((), ()))
CONTRACT_FIRST = (((0,), (0,)), ((), ()))


def rank_matrix(labels, bag, bag_rows):
    rows = labels.shape[1]
    inside = (labels >= bag * bag_rows) & (labels < (bag + 1) * bag_rows)
    earlier = lax.broadcasted_iota(jnp.int32, (rows, rows), 0) < lax.broadcasted_iota(
        jnp.int32, (rows, rows), 1
    )
    ranks = jnp.dot(
        jnp.where(inside, 1.0, 0.0).astype(BF16),
        jnp.where(earlier, 1.0, 0.0).astype(BF16),
        preferred_element_type=F32,
    )
    ranks = jnp.where(inside, ranks, -1.0)[0:1, :]
    slots = lax.broadcasted_iota(jnp.int32, (CAP, rows), 0).astype(F32)
    return jnp.where(slots == ranks, 1.0, 0.0).astype(BF16)


def kernel(
    bags,
    groups,
    heads,
    early,
    block,
    dout_ref,
    labels_ref,
    q_ref,
    k_ref,
    v_ref,
    seq_row_ref,
    seq_col_ref,
    dq_ref,
    dk_ref,
    dv_ref,
    packed,
    arrived,
    other_labels,
    grad_rows,
    qb,
    kb,
    vb,
    gb,
    dqb,
    dkb,
    dvb,
    dk_sum,
    dv_sum,
    in_send,
    in_recv,
    out_send,
    out_recv,
    bag_send,
    bag_recv,
    label_send,
    label_recv,
):
    my_bag = lax.axis_index("bag")
    me = lax.axis_index("head")
    rows, width = dout_ref.shape
    bag_rows = rows * groups
    local = heads * HEAD_DIM
    my_rows = pl.ds(pl.multiple_of(me * rows, rows), rows)

    barrier = pltpu.get_barrier_semaphore()
    for t in range(1, groups):
        pl.semaphore_signal(
            barrier, inc=1, device_id=(my_bag, lax.rem(me + t, groups)), device_id_type=MESH
        )
    for t in range(1, bags):
        pl.semaphore_signal(
            barrier, inc=1, device_id=(lax.rem(my_bag + t, bags), me), device_id_type=MESH
        )
    pl.semaphore_wait(barrier, groups + bags - 2)

    def columns(owner, h):
        return pl.ds(pl.multiple_of(owner * local + h * HEAD_DIM, HEAD_DIM), HEAD_DIM)

    def send_head(source, target, index, h):
        for t in range(1, groups):
            peer = lax.rem(me + t, groups)
            pltpu.make_async_remote_copy(
                src_ref=source.at[:, columns(peer, h)],
                dst_ref=target.at[h, my_rows, :],
                send_sem=in_send.at[index],
                recv_sem=in_recv.at[index, h],
                device_id=(my_bag, peer),
                device_id_type=MESH,
            ).start()
        pltpu.make_async_copy(
            source.at[:, columns(me, h)], target.at[h, my_rows, :], in_recv.at[index, h]
        ).start()

    def send_qkv(h, carry):
        send_head(q_ref, qb, 0, h)
        send_head(k_ref, kb, 1, h)
        send_head(v_ref, vb, 2, h)
        return carry

    lax.fori_loop(0, 1, send_qkv, 0)

    label_copies, bag_copies = [], []
    labels = labels_ref[...]
    for t in range(1, bags):
        copy = pltpu.make_async_remote_copy(
            src_ref=labels_ref,
            dst_ref=other_labels.at[t - 1],
            send_sem=label_send.at[t - 1],
            recv_sem=label_recv.at[t - 1],
            device_id=(lax.rem(my_bag + t, bags), me),
            device_id_type=MESH,
        )
        copy.start()
        label_copies.append(copy)
    for t in list(range(1, bags)) + [0]:
        bag = lax.rem(my_bag + t, bags)
        pick = rank_matrix(labels, bag, bag_rows)

        def pack(i, carry):
            cols = pl.ds(pl.multiple_of(i * local, local), local)
            packed[t, :, cols] = jnp.dot(
                pick, dout_ref[:, cols], preferred_element_type=F32
            ).astype(BF16)
            return carry

        lax.fori_loop(0, width // local, pack, 0)
        if t:
            copy = pltpu.make_async_remote_copy(
                src_ref=packed.at[t],
                dst_ref=arrived.at[t - 1],
                send_sem=bag_send.at[t - 1],
                recv_sem=bag_recv.at[t - 1],
                device_id=(bag, me),
                device_id_type=MESH,
            )
            copy.start()
            bag_copies.append(copy)

    lax.fori_loop(1, early, send_qkv, 0)

    first_row = my_bag * bag_rows + me * rows
    row_ids = first_row + lax.broadcasted_iota(jnp.int32, (rows, rows), 0)
    places = []
    for t in range(bags):
        if t:
            label_copies[t - 1].wait()
            theirs = other_labels[t - 1]
        else:
            theirs = labels
        hit = jnp.where(row_ids == theirs[0:1, :], 1.0, 0.0).astype(BF16)
        places.append(
            lax.dot_general(
                hit,
                rank_matrix(theirs, my_bag, bag_rows),
                CONTRACT_LAST,
                preferred_element_type=F32,
            ).astype(BF16)
        )
    for copy in bag_copies:
        copy.wait()

    def place(i, carry):
        cols = pl.ds(pl.multiple_of(i * local, local), local)
        total = jnp.dot(places[0], packed[0, :, cols], preferred_element_type=F32)
        for t in range(1, bags):
            total += jnp.dot(places[t], arrived[t - 1, :, cols], preferred_element_type=F32)
        grad_rows[:, cols] = total.astype(BF16)
        return carry

    lax.fori_loop(0, width // local, place, 0)

    def send_grad(h, carry):
        send_head(grad_rows, gb, 3, h)
        return carry

    def send_all(h, carry):
        return send_grad(h, send_qkv(h, carry))

    lax.fori_loop(0, early, send_grad, 0)
    lax.fori_loop(early, heads, send_all, 0)

    scale = HEAD_DIM ** (-0.5)
    exp2_scale = scale * 1.4426950408889634

    def one_head(h, carry):
        for index, buffer in enumerate((qb, kb, vb, gb)):
            pltpu.make_async_copy(buffer.at[h], buffer.at[h], in_recv.at[index, h]).wait()
        dk_sum[...] = jnp.zeros_like(dk_sum)
        dv_sum[...] = jnp.zeros_like(dv_sum)

        def one_block(i, inner):
            here = pl.ds(pl.multiple_of(i * block, block), block)
            query, grad = qb[h, here, :], gb[h, here, :]
            keys, values = kb[h], vb[h]
            scores = lax.dot_general(keys, query, CONTRACT_LAST, preferred_element_type=F32)
            same = seq_col_ref[...] == seq_row_ref[:, here]
            scores = jnp.where(same, scores, -jnp.inf)
            top = jnp.max(scores, axis=0, keepdims=True)
            exponent = jnp.exp2((scores - top) * exp2_scale)
            probs = exponent * (1.0 / jnp.sum(exponent, axis=0, keepdims=True))
            dv_sum[...] += jnp.dot(probs.astype(BF16), grad, preferred_element_type=F32)
            dprobs = lax.dot_general(values, grad, CONTRACT_LAST, preferred_element_type=F32)
            delta = jnp.sum(probs * dprobs, axis=0, keepdims=True)
            dscores = (probs * (dprobs - delta) * scale).astype(BF16)
            dk_sum[...] += jnp.dot(dscores, query, preferred_element_type=F32)
            dqb[h, here, :] = lax.dot_general(
                dscores, keys, CONTRACT_FIRST, preferred_element_type=F32
            ).astype(BF16)
            return inner

        lax.fori_loop(0, bag_rows // block, one_block, 0)
        dkb[h] = dk_sum[...].astype(BF16)
        dvb[h] = dv_sum[...].astype(BF16)
        for index, (source, target) in enumerate(((dqb, dq_ref), (dkb, dk_ref), (dvb, dv_ref))):
            for t in range(1, groups):
                peer = lax.rem(me + t, groups)
                theirs = pl.ds(pl.multiple_of(peer * rows, rows), rows)
                pltpu.make_async_remote_copy(
                    src_ref=source.at[h, theirs, :],
                    dst_ref=target.at[:, columns(me, h)],
                    send_sem=out_send.at[index],
                    recv_sem=out_recv.at[index],
                    device_id=(my_bag, peer),
                    device_id_type=MESH,
                ).start()
            pltpu.make_async_copy(
                source.at[h, my_rows, :], target.at[:, columns(me, h)], out_recv.at[index]
            ).start()
        return carry

    lax.fori_loop(0, heads, one_head, 0)

    sent = grad_rows.at[:, pl.ds(0, (groups - 1) * local)]
    for index in range(4):
        pltpu.make_async_copy(sent, sent, in_send.at[index]).wait()
    for index, target in enumerate((dq_ref, dk_ref, dv_ref)):
        pltpu.make_async_copy(sent, sent, out_send.at[index]).wait()
        pltpu.make_async_copy(target, target, out_recv.at[index]).wait()


def per_device(dout, destination, q_bag, k_bag, v_bag, seq_ids):
    rows, width = dout.shape
    bags = lax.axis_size("bag")
    groups = lax.axis_size("head")
    bag_rows = rows * groups
    heads = width // HEAD_DIM // groups
    early = (heads + 1) // 2
    block = min(256, bag_rows)
    labels = jnp.broadcast_to(destination[None, :], (8, rows))
    whole = pl.BlockSpec(memory_space=pltpu.VMEM)
    far = pl.BlockSpec(memory_space=pl.ANY)
    sems = pltpu.SemaphoreType.DMA
    head_buffer = pltpu.VMEM((heads, bag_rows, HEAD_DIM), BF16)
    return pl.pallas_call(
        functools.partial(kernel, bags, groups, heads, early, block),
        out_shape=[jax.ShapeDtypeStruct((rows, width), BF16)] * 3,
        in_specs=[whole, whole, far, far, far, whole, whole],
        out_specs=[far, far, far],
        scratch_shapes=[
            pltpu.VMEM((bags, CAP, width), BF16),
            pltpu.VMEM((bags - 1, CAP, width), BF16),
            pltpu.VMEM((bags - 1, 8, rows), jnp.int32),
            pltpu.VMEM((rows, width), BF16),
        ]
        + [head_buffer] * 7
        + [
            pltpu.VMEM((bag_rows, HEAD_DIM), F32),
            pltpu.VMEM((bag_rows, HEAD_DIM), F32),
            sems((4,)),
            sems((4, heads)),
            sems((3,)),
            sems((3,)),
            sems((bags - 1,)),
            sems((bags - 1,)),
            sems((bags - 1,)),
            sems((bags - 1,)),
        ],
        compiler_params=pltpu.CompilerParams(
            collective_id=0, has_side_effects=True, vmem_limit_bytes=56 * 1024 * 1024
        ),
    )(dout, labels, q_bag, k_bag, v_bag, seq_ids, seq_ids.reshape(bag_rows, 1))


def solution(mesh):
    placed = (
        P(("bag", "head"), None),
        P(("bag", "head")),
        P(("bag", "head"), None),
        P(("bag", "head"), None),
        P(("bag", "head"), None),
        P("bag", None),
    )
    return jax.shard_map(
        per_device,
        mesh=mesh,
        in_specs=placed,
        out_specs=(P(("bag", "head"), None),) * 3,
        check_vma=False,
    )
```

```python
import functools

import jax
import jax.numpy as jnp
from jax import lax
from jax.experimental import pallas as pl
from jax.experimental.pallas import tpu as pltpu
from jax.sharding import PartitionSpec as P

HEAD_DIM = 128
CAP = 64
MESH = pl.DeviceIdType.MESH
F32 = jnp.float32
BF16 = jnp.bfloat16
NEVER = -1e30
CONTRACT_LAST = (((1,), (1,)), ((), ()))
CONTRACT_FIRST = (((0,), (0,)), ((), ()))


def rank_matrix(labels, bag, bag_rows):
    rows = labels.shape[1]
    inside = (labels >= bag * bag_rows) & (labels < (bag + 1) * bag_rows)
    earlier = lax.broadcasted_iota(jnp.int32, (rows, rows), 0) < lax.broadcasted_iota(
        jnp.int32, (rows, rows), 1
    )
    ranks = jnp.dot(
        jnp.where(inside, 1.0, 0.0).astype(BF16),
        jnp.where(earlier, 1.0, 0.0).astype(BF16),
        preferred_element_type=F32,
    )
    ranks = jnp.where(inside, ranks, -1.0)[0:1, :]
    slots = lax.broadcasted_iota(jnp.int32, (CAP, rows), 0).astype(F32)
    return jnp.where(slots == ranks, 1.0, 0.0).astype(BF16)


def kernel(
    bags,
    groups,
    heads,
    early,
    block,
    dout_ref,
    labels_ref,
    q_ref,
    k_ref,
    v_ref,
    seq_row_ref,
    seq_col_ref,
    dq_ref,
    dk_ref,
    dv_ref,
    packed,
    arrived,
    other_labels,
    grad_rows,
    qb,
    gb,
    kb,
    vb,
    dq_own,
    dq_out,
    dq_in,
    dqb,
    dkb,
    dvb,
    my_stats,
    pair_stats,
    dk_sum,
    dv_sum,
    in_send,
    in_recv,
    pair_send,
    pair_recv,
    stat_send,
    stat_recv,
    part_send,
    part_recv,
    out_send,
    out_recv,
    bag_send,
    bag_recv,
    label_send,
    label_recv,
):
    my_bag = lax.axis_index("bag")
    me = lax.axis_index("head")
    half = groups // 2
    side = me // half
    place_in = lax.rem(me, half)
    partner = (my_bag, lax.rem(me + half, groups))
    rows, width = dout_ref.shape
    bag_rows = rows * groups
    half_rows = rows * half
    local = heads * HEAD_DIM
    my_rows = pl.ds(pl.multiple_of(place_in * rows, rows), rows)

    def mate(t):
        at = lax.rem(place_in + t, half)
        return at, (my_bag, side * half + at)

    barrier = pltpu.get_barrier_semaphore()
    for t in range(1, half):
        pl.semaphore_signal(barrier, inc=1, device_id=mate(t)[1], device_id_type=MESH)
    pl.semaphore_signal(barrier, inc=1, device_id=partner, device_id_type=MESH)
    for t in range(1, bags):
        pl.semaphore_signal(
            barrier, inc=1, device_id=(lax.rem(my_bag + t, bags), me), device_id_type=MESH
        )
    pl.semaphore_wait(barrier, half + bags - 1)

    def columns(owner, h):
        return pl.ds(pl.multiple_of(owner * local + h * HEAD_DIM, HEAD_DIM), HEAD_DIM)

    def send_head(source, target, index, h):
        for t in range(1, half):
            at, device = mate(t)
            pltpu.make_async_remote_copy(
                src_ref=source.at[:, columns(at, h)],
                dst_ref=target.at[h, my_rows, :],
                send_sem=in_send.at[index],
                recv_sem=in_recv.at[index, h],
                device_id=device,
                device_id_type=MESH,
            ).start()
        pltpu.make_async_copy(
            source.at[:, columns(place_in, h)], target.at[h, my_rows, :], in_recv.at[index, h]
        ).start()

    def wait_head(buffer, index, h):
        pltpu.make_async_copy(buffer.at[h], buffer.at[h], in_recv.at[index, h]).wait()

    def to_partner(source, target, send_sem, recv_sem):
        pltpu.make_async_remote_copy(
            src_ref=source,
            dst_ref=target,
            send_sem=send_sem,
            recv_sem=recv_sem,
            device_id=partner,
            device_id_type=MESH,
        ).start()

    def send_q(h, carry):
        send_head(q_ref, qb.at[0], 0, h)
        return carry

    def send_kv(h, carry):
        send_head(k_ref, kb, 1, h)
        send_head(v_ref, vb, 2, h)
        return carry

    def send_grad(h, carry):
        send_head(grad_rows, gb.at[0], 3, h)
        return carry

    def relay_q(h, carry):
        wait_head(qb.at[0], 0, h)
        to_partner(qb.at[0, h], qb.at[1, h], pair_send.at[0], pair_recv.at[0, h])
        return carry

    def relay_grad(h, carry):
        wait_head(gb.at[0], 3, h)
        to_partner(gb.at[0, h], gb.at[1, h], pair_send.at[1], pair_recv.at[1, h])
        return carry

    lax.fori_loop(0, heads, send_q, 0)

    label_copies, bag_copies = [], []
    labels = labels_ref[...]
    for t in range(1, bags):
        copy = pltpu.make_async_remote_copy(
            src_ref=labels_ref,
            dst_ref=other_labels.at[t - 1],
            send_sem=label_send.at[t - 1],
            recv_sem=label_recv.at[t - 1],
            device_id=(lax.rem(my_bag + t, bags), me),
            device_id_type=MESH,
        )
        copy.start()
        label_copies.append(copy)
    for t in list(range(1, bags)) + [0]:
        bag = lax.rem(my_bag + t, bags)
        pick = rank_matrix(labels, bag, bag_rows)

        def pack(i, carry):
            cols = pl.ds(pl.multiple_of(i * local, local), local)
            packed[t, :, cols] = jnp.dot(
                pick, dout_ref[:, cols], preferred_element_type=F32
            ).astype(BF16)
            return carry

        lax.fori_loop(0, width // local, pack, 0)
        if t:
            copy = pltpu.make_async_remote_copy(
                src_ref=packed.at[t],
                dst_ref=arrived.at[t - 1],
                send_sem=bag_send.at[t - 1],
                recv_sem=bag_recv.at[t - 1],
                device_id=(bag, me),
                device_id_type=MESH,
            )
            copy.start()
            bag_copies.append(copy)

    lax.fori_loop(0, early, relay_q, 0)
    lax.fori_loop(0, early, send_kv, 0)
    lax.fori_loop(early, heads, relay_q, 0)

    first_row = my_bag * bag_rows + me * rows
    row_ids = first_row + lax.broadcasted_iota(jnp.int32, (rows, rows), 0)
    places = []
    for t in range(bags):
        if t:
            label_copies[t - 1].wait()
            theirs = other_labels[t - 1]
        else:
            theirs = labels
        hit = jnp.where(row_ids == theirs[0:1, :], 1.0, 0.0).astype(BF16)
        places.append(
            lax.dot_general(
                hit,
                rank_matrix(theirs, my_bag, bag_rows),
                CONTRACT_LAST,
                preferred_element_type=F32,
            ).astype(BF16)
        )
    for copy in bag_copies:
        copy.wait()

    def place(i, carry):
        cols = pl.ds(pl.multiple_of(i * local, local), local)
        total = jnp.dot(places[0], packed[0, :, cols], preferred_element_type=F32)
        for t in range(1, bags):
            total += jnp.dot(places[t], arrived[t - 1, :, cols], preferred_element_type=F32)
        grad_rows[:, cols] = total.astype(BF16)
        return carry

    lax.fori_loop(0, width // local, place, 0)

    lax.fori_loop(0, heads, send_grad, 0)
    lax.fori_loop(early, heads, send_kv, 0)

    scale = HEAD_DIM ** (-0.5)
    exp2_scale = scale * 1.4426950408889634
    blocks = half_rows // block
    key_labels = seq_col_ref.at[pl.ds(pl.multiple_of(side * half_rows, half_rows), half_rows), :]

    def block_parts(part, i, h):
        here = pl.ds(pl.multiple_of(i * block, block), block)
        other = side + part - 2 * side * part
        query_at = pl.ds(pl.multiple_of(other * half_rows + i * block, block), block)
        query, grad = qb[part, h, here, :], gb[part, h, here, :]
        scores = lax.dot_general(kb[h], query, CONTRACT_LAST, preferred_element_type=F32)
        scores = jnp.where(key_labels[...] == seq_row_ref[:, query_at], scores, NEVER)
        dprobs = lax.dot_general(vb[h], grad, CONTRACT_LAST, preferred_element_type=F32)
        return here, query_at, query, grad, scores, dprobs

    def statistics(h):
        wait_head(kb, 1, h)
        wait_head(vb, 2, h)
        for index, buffer in enumerate((qb, gb)):
            ref = buffer.at[1, h]
            pltpu.make_async_copy(ref, ref, pair_recv.at[index, h]).wait()

        for part in (1, 0):

            def one_block(i, inner):
                _, query_at, _, _, scores, dprobs = block_parts(part, i, h)
                top = jnp.max(scores, axis=0, keepdims=True)
                exponent = jnp.exp2((scores - top) * exp2_scale)
                my_stats[h, 0:1, query_at] = top
                my_stats[h, 1:2, query_at] = jnp.sum(exponent, axis=0, keepdims=True)
                my_stats[h, 2:3, query_at] = jnp.sum(exponent * dprobs, axis=0, keepdims=True)
                return inner

            lax.fori_loop(0, blocks, one_block, 0)
        to_partner(my_stats.at[h], pair_stats.at[h], stat_send.at[0], stat_recv.at[h])

    def send_out(source, target, index, h):
        for t in range(1, half):
            at, device = mate(t)
            theirs = pl.ds(pl.multiple_of(at * rows, rows), rows)
            pltpu.make_async_remote_copy(
                src_ref=source.at[h, theirs, :],
                dst_ref=target.at[:, columns(place_in, h)],
                send_sem=out_send.at[index],
                recv_sem=out_recv.at[index],
                device_id=device,
                device_id_type=MESH,
            ).start()
        pltpu.make_async_copy(
            source.at[h, my_rows, :], target.at[:, columns(place_in, h)], out_recv.at[index]
        ).start()

    def gradients(h):
        stats = pair_stats.at[h]
        pltpu.make_async_copy(stats, stats, stat_recv.at[h]).wait()
        dk_sum[...] = jnp.zeros_like(dk_sum)
        dv_sum[...] = jnp.zeros_like(dv_sum)

        for part in (1, 0):

            def one_block(i, inner):
                here, query_at, query, grad, scores, dprobs = block_parts(part, i, h)
                top_a, top_b = my_stats[h, 0:1, query_at], pair_stats[h, 0:1, query_at]
                top = jnp.maximum(top_a, top_b)
                weight_a = jnp.exp2((top_a - top) * exp2_scale)
                weight_b = jnp.exp2((top_b - top) * exp2_scale)
                inverse = 1.0 / (
                    my_stats[h, 1:2, query_at] * weight_a + pair_stats[h, 1:2, query_at] * weight_b
                )
                delta = inverse * (
                    my_stats[h, 2:3, query_at] * weight_a + pair_stats[h, 2:3, query_at] * weight_b
                )
                probs = jnp.exp2((scores - top) * exp2_scale) * inverse
                dv_sum[...] += jnp.dot(probs.astype(BF16), grad, preferred_element_type=F32)
                dscores = (probs * (dprobs - delta)).astype(BF16)
                dk_sum[...] += jnp.dot(dscores, query, preferred_element_type=F32)
                dq = scale * lax.dot_general(
                    dscores, kb[h], CONTRACT_FIRST, preferred_element_type=F32
                )
                if part:
                    dq_out[h, here, :] = dq.astype(BF16)
                else:
                    dq_own[h, here, :] = dq
                return inner

            lax.fori_loop(0, blocks, one_block, 0)
            if part:
                to_partner(dq_out.at[h], dq_in.at[h], part_send.at[0], part_recv.at[h])
        dkb[h] = (dk_sum[...] * scale).astype(BF16)
        dvb[h] = dv_sum[...].astype(BF16)
        send_out(dkb, dk_ref, 1, h)
        send_out(dvb, dv_ref, 2, h)

    def finish(h):
        part = dq_in.at[h]
        pltpu.make_async_copy(part, part, part_recv.at[h]).wait()
        dqb[h] = (dq_own[h] + dq_in[h].astype(F32)).astype(BF16)
        send_out(dqb, dq_ref, 0, h)

    ahead, lag = min(3, heads), min(2, heads)
    lax.fori_loop(0, ahead, relay_grad, 0)
    statistics(0)

    def step(h, carry):
        @pl.when(h + ahead < heads)
        def _():
            relay_grad(h + ahead, 0)

        @pl.when(h + 1 < heads)
        def _():
            statistics(h + 1)

        gradients(h)

        @pl.when(h >= lag)
        def _():
            finish(h - lag)

        return carry

    lax.fori_loop(0, heads, step, 0)

    def last(h, carry):
        finish(h)
        return carry

    lax.fori_loop(heads - lag, heads, last, 0)

    sent = grad_rows.at[:, pl.ds(0, (half - 1) * local)]
    for index in range(4):
        pltpu.make_async_copy(sent, sent, in_send.at[index]).wait()
    for index in range(2):
        pltpu.make_async_copy(dq_out, dq_out, pair_send.at[index]).wait()
    pltpu.make_async_copy(dq_out, dq_out, part_send.at[0]).wait()
    pltpu.make_async_copy(my_stats, my_stats, stat_send.at[0]).wait()
    for index, target in enumerate((dq_ref, dk_ref, dv_ref)):
        pltpu.make_async_copy(sent, sent, out_send.at[index]).wait()
        pltpu.make_async_copy(target, target, out_recv.at[index]).wait()


def per_device(dout, destination, q_bag, k_bag, v_bag, seq_ids):
    rows, width = dout.shape
    bags = lax.axis_size("bag")
    groups = lax.axis_size("head")
    half = groups // 2
    bag_rows = rows * groups
    half_rows = rows * half
    heads = width // HEAD_DIM // half
    early = (heads + 2) // 3
    block = min(256, half_rows)
    labels = jnp.broadcast_to(destination[None, :], (8, rows))
    whole = pl.BlockSpec(memory_space=pltpu.VMEM)
    far = pl.BlockSpec(memory_space=pl.ANY)
    sems = pltpu.SemaphoreType.DMA
    one = pltpu.VMEM((heads, half_rows, HEAD_DIM), BF16)
    two = pltpu.VMEM((2, heads, half_rows, HEAD_DIM), BF16)
    return pl.pallas_call(
        functools.partial(kernel, bags, groups, heads, early, block),
        out_shape=[jax.ShapeDtypeStruct((rows, width), BF16)] * 3,
        in_specs=[whole, whole, far, far, far, whole, whole],
        out_specs=[far, far, far],
        scratch_shapes=[
            pltpu.VMEM((bags, CAP, width), BF16),
            pltpu.VMEM((bags - 1, CAP, width), BF16),
            pltpu.VMEM((bags - 1, 8, rows), jnp.int32),
            pltpu.VMEM((rows, width), BF16),
            two,
            two,
            one,
            one,
            pltpu.VMEM((heads, half_rows, HEAD_DIM), F32),
            one,
            one,
            one,
            one,
            one,
            pltpu.VMEM((heads, 8, bag_rows), F32),
            pltpu.VMEM((heads, 8, bag_rows), F32),
            pltpu.VMEM((half_rows, HEAD_DIM), F32),
            pltpu.VMEM((half_rows, HEAD_DIM), F32),
            sems((4,)),
            sems((4, heads)),
            sems((2,)),
            sems((2, heads)),
            sems((1,)),
            sems((heads,)),
            sems((1,)),
            sems((heads,)),
            sems((3,)),
            sems((3,)),
            sems((bags - 1,)),
            sems((bags - 1,)),
            sems((bags - 1,)),
            sems((bags - 1,)),
        ],
        compiler_params=pltpu.CompilerParams(
            collective_id=0, has_side_effects=True, vmem_limit_bytes=56 * 1024 * 1024
        ),
    )(dout, labels, q_bag, k_bag, v_bag, seq_ids, seq_ids.reshape(bag_rows, 1))


def solution(mesh):
    placed = (
        P(("bag", "head"), None),
        P(("bag", "head")),
        P(("bag", "head"), None),
        P(("bag", "head"), None),
        P(("bag", "head"), None),
        P("bag", None),
    )
    return jax.shard_map(
        per_device,
        mesh=mesh,
        in_specs=placed,
        out_specs=(P(("bag", "head"), None),) * 3,
        check_vma=False,
    )
```

```python
import functools

import jax
import jax.numpy as jnp
from jax import lax
from jax.experimental import pallas as pl
from jax.experimental.pallas import tpu as pltpu
from jax.sharding import PartitionSpec as P

HEAD_DIM = 128
CAP = 64
MESH = pl.DeviceIdType.MESH
F32 = jnp.float32
BF16 = jnp.bfloat16
CONTRACT_LAST = (((1,), (1,)), ((), ()))
CONTRACT_FIRST = (((0,), (0,)), ((), ()))


def rank_matrix(labels, bag, bag_rows):
    rows = labels.shape[1]
    inside = (labels >= bag * bag_rows) & (labels < (bag + 1) * bag_rows)
    earlier = lax.broadcasted_iota(jnp.int32, (rows, rows), 0) < lax.broadcasted_iota(
        jnp.int32, (rows, rows), 1
    )
    ranks = jnp.dot(
        jnp.where(inside, 1.0, 0.0).astype(BF16),
        jnp.where(earlier, 1.0, 0.0).astype(BF16),
        preferred_element_type=F32,
    )
    ranks = jnp.where(inside, ranks, -1.0)[0:1, :]
    slots = lax.broadcasted_iota(jnp.int32, (CAP, rows), 0).astype(F32)
    return jnp.where(slots == ranks, 1.0, 0.0).astype(BF16)


def kernel(
    bags,
    groups,
    heads,
    early,
    block,
    dout_ref,
    home_ref,
    q_ref,
    k_ref,
    v_ref,
    seq_row_ref,
    dq_ref,
    dk_ref,
    dv_ref,
    packed,
    arrived,
    other_labels,
    grad_rows,
    qb,
    kb,
    vb,
    gb,
    dqb,
    dkb,
    dvb,
    dk_sum,
    dv_sum,
    labels_ref,
    seq_col_ref,
    in_send,
    in_recv,
    out_send,
    out_recv,
    bag_send,
    bag_recv,
    label_send,
    label_recv,
):
    my_bag = lax.axis_index("bag")
    me = lax.axis_index("head")
    rows, width = dout_ref.shape
    bag_rows = rows * groups
    local = heads * HEAD_DIM
    my_rows = pl.ds(pl.multiple_of(me * rows, rows), rows)

    barrier = pltpu.get_barrier_semaphore()
    for t in range(1, groups):
        pl.semaphore_signal(
            barrier, inc=1, device_id=(my_bag, lax.rem(me + t, groups)), device_id_type=MESH
        )
    for t in range(1, bags):
        pl.semaphore_signal(
            barrier, inc=1, device_id=(lax.rem(my_bag + t, bags), me), device_id_type=MESH
        )
    pl.semaphore_wait(barrier, groups + bags - 2)

    def columns(owner, h):
        return pl.ds(pl.multiple_of(owner * local + h * HEAD_DIM, HEAD_DIM), HEAD_DIM)

    def send_head(source, target, index, h):
        for t in range(1, groups):
            peer = lax.rem(me + t, groups)
            pltpu.make_async_remote_copy(
                src_ref=source.at[:, columns(peer, h)],
                dst_ref=target.at[h, my_rows, :],
                send_sem=in_send.at[index],
                recv_sem=in_recv.at[index, h],
                device_id=(my_bag, peer),
                device_id_type=MESH,
            ).start()
        pltpu.make_async_copy(
            source.at[:, columns(me, h)], target.at[h, my_rows, :], in_recv.at[index, h]
        ).start()

    def send_qkv(h, carry):
        send_head(q_ref, qb, 0, h)
        send_head(k_ref, kb, 1, h)
        send_head(v_ref, vb, 2, h)
        return carry

    lax.fori_loop(0, 1, send_qkv, 0)

    labels_ref[...] = jnp.broadcast_to(home_ref[...], labels_ref.shape)
    diagonal = lax.broadcasted_iota(jnp.int32, (rows, rows), 0) == lax.broadcasted_iota(
        jnp.int32, (rows, rows), 1
    )
    for g in range(groups):
        span = pl.ds(g * rows, rows)
        seq_col_ref[span, :] = jnp.sum(
            jnp.where(diagonal, seq_row_ref[:, span], 0), axis=1, keepdims=True
        )

    label_copies, bag_copies = [], []
    labels = labels_ref[...]
    for t in range(1, bags):
        copy = pltpu.make_async_remote_copy(
            src_ref=labels_ref,
            dst_ref=other_labels.at[t - 1],
            send_sem=label_send.at[t - 1],
            recv_sem=label_recv.at[t - 1],
            device_id=(lax.rem(my_bag + t, bags), me),
            device_id_type=MESH,
        )
        copy.start()
        label_copies.append(copy)
    for t in list(range(1, bags)) + [0]:
        bag = lax.rem(my_bag + t, bags)
        pick = rank_matrix(labels, bag, bag_rows)

        def pack(i, carry):
            cols = pl.ds(pl.multiple_of(i * local, local), local)
            packed[t, :, cols] = jnp.dot(
                pick, dout_ref[:, cols], preferred_element_type=F32
            ).astype(BF16)
            return carry

        lax.fori_loop(0, width // local, pack, 0)
        if t:
            copy = pltpu.make_async_remote_copy(
                src_ref=packed.at[t],
                dst_ref=arrived.at[t - 1],
                send_sem=bag_send.at[t - 1],
                recv_sem=bag_recv.at[t - 1],
                device_id=(bag, me),
                device_id_type=MESH,
            )
            copy.start()
            bag_copies.append(copy)

    lax.fori_loop(1, early, send_qkv, 0)

    first_row = my_bag * bag_rows + me * rows
    row_ids = first_row + lax.broadcasted_iota(jnp.int32, (rows, rows), 0)
    places = []
    for t in range(bags):
        if t:
            label_copies[t - 1].wait()
            theirs = other_labels[t - 1]
        else:
            theirs = labels
        hit = jnp.where(row_ids == theirs[0:1, :], 1.0, 0.0).astype(BF16)
        places.append(
            lax.dot_general(
                hit,
                rank_matrix(theirs, my_bag, bag_rows),
                CONTRACT_LAST,
                preferred_element_type=F32,
            ).astype(BF16)
        )
    for copy in bag_copies:
        copy.wait()

    def place(i, carry):
        cols = pl.ds(pl.multiple_of(i * local, local), local)
        total = jnp.dot(places[0], packed[0, :, cols], preferred_element_type=F32)
        for t in range(1, bags):
            total += jnp.dot(places[t], arrived[t - 1, :, cols], preferred_element_type=F32)
        grad_rows[:, cols] = total.astype(BF16)
        return carry

    lax.fori_loop(0, width // local, place, 0)

    def send_grad(h, carry):
        send_head(grad_rows, gb, 3, h)
        return carry

    def send_all(h, carry):
        return send_grad(h, send_qkv(h, carry))

    lax.fori_loop(0, early, send_grad, 0)
    lax.fori_loop(early, heads, send_all, 0)

    scale = HEAD_DIM ** (-0.5)
    exp2_scale = scale * 1.4426950408889634

    def one_head(h, carry):
        for index, buffer in enumerate((qb, kb, vb, gb)):
            pltpu.make_async_copy(buffer.at[h], buffer.at[h], in_recv.at[index, h]).wait()
        dk_sum[...] = jnp.zeros_like(dk_sum)
        dv_sum[...] = jnp.zeros_like(dv_sum)

        def one_block(i, inner):
            here = pl.ds(pl.multiple_of(i * block, block), block)
            query, grad = qb[h, here, :], gb[h, here, :]
            keys, values = kb[h], vb[h]
            scores = lax.dot_general(keys, query, CONTRACT_LAST, preferred_element_type=F32)
            same = seq_col_ref[...] == seq_row_ref[:, here]
            scores = jnp.where(same, scores, -jnp.inf)
            top = jnp.max(scores, axis=0, keepdims=True)
            exponent = jnp.exp2((scores - top) * exp2_scale)
            probs = exponent * (1.0 / jnp.sum(exponent, axis=0, keepdims=True))
            dv_sum[...] += jnp.dot(probs.astype(BF16), grad, preferred_element_type=F32)
            dprobs = lax.dot_general(values, grad, CONTRACT_LAST, preferred_element_type=F32)
            delta = jnp.sum(probs * dprobs, axis=0, keepdims=True)
            dscores = (probs * (dprobs - delta) * scale).astype(BF16)
            dk_sum[...] += jnp.dot(dscores, query, preferred_element_type=F32)
            dqb[h, here, :] = lax.dot_general(
                dscores, keys, CONTRACT_FIRST, preferred_element_type=F32
            ).astype(BF16)
            return inner

        lax.fori_loop(0, bag_rows // block, one_block, 0)
        dkb[h] = dk_sum[...].astype(BF16)
        dvb[h] = dv_sum[...].astype(BF16)
        for index, (source, target) in enumerate(((dqb, dq_ref), (dkb, dk_ref), (dvb, dv_ref))):
            for t in range(1, groups):
                peer = lax.rem(me + t, groups)
                theirs = pl.ds(pl.multiple_of(peer * rows, rows), rows)
                pltpu.make_async_remote_copy(
                    src_ref=source.at[h, theirs, :],
                    dst_ref=target.at[:, columns(me, h)],
                    send_sem=out_send.at[index],
                    recv_sem=out_recv.at[index],
                    device_id=(my_bag, peer),
                    device_id_type=MESH,
                ).start()
            pltpu.make_async_copy(
                source.at[h, my_rows, :], target.at[:, columns(me, h)], out_recv.at[index]
            ).start()
        return carry

    lax.fori_loop(0, heads, one_head, 0)

    sent = grad_rows.at[:, pl.ds(0, (groups - 1) * local)]
    for index in range(4):
        pltpu.make_async_copy(sent, sent, in_send.at[index]).wait()
    for index, target in enumerate((dq_ref, dk_ref, dv_ref)):
        pltpu.make_async_copy(sent, sent, out_send.at[index]).wait()
        pltpu.make_async_copy(target, target, out_recv.at[index]).wait()


def per_device(dout, destination, q_bag, k_bag, v_bag, seq_ids):
    rows, width = dout.shape
    bags = lax.axis_size("bag")
    groups = lax.axis_size("head")
    bag_rows = rows * groups
    heads = width // HEAD_DIM // groups
    early = (heads + 1) // 2
    block = min(256, bag_rows)
    whole = pl.BlockSpec(memory_space=pltpu.VMEM)
    far = pl.BlockSpec(memory_space=pl.ANY)
    sems = pltpu.SemaphoreType.DMA
    head_buffer = pltpu.VMEM((heads, bag_rows, HEAD_DIM), BF16)
    return pl.pallas_call(
        functools.partial(kernel, bags, groups, heads, early, block),
        out_shape=[jax.ShapeDtypeStruct((rows, width), BF16)] * 3,
        in_specs=[whole, whole, far, far, far, whole],
        out_specs=[far, far, far],
        scratch_shapes=[
            pltpu.VMEM((bags, CAP, width), BF16),
            pltpu.VMEM((bags - 1, CAP, width), BF16),
            pltpu.VMEM((bags - 1, 8, rows), jnp.int32),
            pltpu.VMEM((rows, width), BF16),
        ]
        + [head_buffer] * 7
        + [
            pltpu.VMEM((bag_rows, HEAD_DIM), F32),
            pltpu.VMEM((bag_rows, HEAD_DIM), F32),
            pltpu.VMEM((8, rows), jnp.int32),
            pltpu.VMEM((bag_rows, 1), jnp.int32),
            sems((4,)),
            sems((4, heads)),
            sems((3,)),
            sems((3,)),
            sems((bags - 1,)),
            sems((bags - 1,)),
            sems((bags - 1,)),
            sems((bags - 1,)),
        ],
        compiler_params=pltpu.CompilerParams(
            collective_id=0, has_side_effects=True, vmem_limit_bytes=56 * 1024 * 1024
        ),
    )(dout, destination[None, :], q_bag, k_bag, v_bag, seq_ids)


def solution(mesh):
    placed = (
        P(("bag", "head"), None),
        P(("bag", "head")),
        P(("bag", "head"), None),
        P(("bag", "head"), None),
        P(("bag", "head"), None),
        P("bag", None),
    )
    return jax.shard_map(
        per_device,
        mesh=mesh,
        in_specs=placed,
        out_specs=(P(("bag", "head"), None),) * 3,
        check_vma=False,
    )
```
